512 devices in a mesh: dp: 64 (over x, z_lo, core), fsdp: 8 (over y, z_hi).
Axes of the slice: x: 4, y: 4, z: 16 (z_hi: 2, z_lo: 8; z = z_hi * 8 + z_lo), core: 2. Of those that a mesh axis runs over, the one named last changes fastest.
Arguments:
- acts: bfloat16 [24576, 8192], P('dp', 'fsdp'), may hold values from -6 to 6
- grad_out: bfloat16 [24576, 8192], P('dp', 'fsdp'), may hold values from -16 to 16
- basis: bfloat16 [8192, 1024], P('fsdp', 'dp'), may hold values from -0.0625 to 0.0625
- master: float32 [8, 1024, 8192], P(None, 'dp', 'fsdp'), may hold values from -4 to 4
- first_mom: float32 [8, 1024, 1024], P('fsdp', 'dp'), may hold values from -2 to 2
- second_mom: float32 [8, 1024, 1024], P('fsdp', 'dp'), may hold values from 0.0001 to 0.01
Outputs:
- new_master: float32 [8, 1024, 8192], P(None, 'dp', 'fsdp')
- forward: bfloat16 [8, 1024, 8192], P(None, 'dp')
- new_first: float32 [8, 1024, 1024], P('fsdp', 'dp')
- new_second: float32 [8, 1024, 1024], P('fsdp', 'dp')
The draws below stay inside these ranges and needn't reach their ends.
All inputs are finite; a program needn't handle non-finite values.
Results may differ from the reference program's by a relative error of at most 0.0021.
Values may be sent and summed in bfloat16 or wider, within the bound.
No kernel may reach another device: no remote copies, remote signals or barrier semaphores. Data moves between devices by JAX's collectives and lax.ppermute only.
A program may use at most 64 MiB of HBM per device.

```python
import math
import jax
import jax.numpy as jnp

D = 8192
R = 1024
TOKENS = 24576
GROUPS = 8
COLS = 1024


def with_spikes(array, key, source, target, blocks, factor):
    owner, partner = [(jnp.arange(array.shape[axis_at]) // (array.shape[axis_at] // blocks)).reshape([-1 if axis == axis_at else 1 for axis in range(array.ndim)]) for axis_at in (source, target)]
    chosen = jax.random.permutation(key, blocks)[partner]
    strong = (owner == chosen) | (owner == (partner + blocks // 2) % blocks)
    return jnp.where(strong, factor * array, array)


def level_of(stream_key, dims, shards, least, largest):
    factor_of = 1.0
    for position, parts in shards:
        steps = jax.random.uniform(jax.random.fold_in(jax.random.fold_in(stream_key, 6), position), (parts,), jnp.float32, least / len(shards), largest / len(shards))
        factor_of = factor_of * jnp.repeat(jnp.exp(steps), dims[position] // parts).reshape((-1,) + (1,) * (len(dims) - 1 - position))
    return factor_of


def gaussian(key, shape, scale, reach, cuts=(), dtype=jnp.bfloat16):
    values = scale * jax.random.normal(key, shape, jnp.float32)
    if cuts:
        values = values * level_of(key, shape, cuts, -0.22, 0.18)
    return jnp.clip(values, -reach, reach).astype(dtype)


def noise_with(rng, shape, deviation, limit, pieces, heavy, held_as=jnp.bfloat16):
    values = deviation * jax.random.normal(rng, shape, jnp.float32)
    if pieces:
        values = values * level_of(rng, shape, pieces, -0.22, 0.18)
    return jnp.clip(with_spikes(values, jax.random.fold_in(rng, 3), *heavy), -limit, limit).astype(held_as)


def setup_inputs(seed: int = 0) -> dict:
    seeds = jax.random.split(jax.random.key(seed), 7)
    acts = gaussian(seeds[0], (TOKENS, D), 1.0, 6.0, ((0, 64), (1, 8)))
    grad_out = noise_with(seeds[1], (TOKENS, D), 1.0, 16.0, ((0, 64), (1, 8)), (0, 1, 64, 4.0))
    basis = gaussian(seeds[2], (D, R), D ** -0.5, 0.0625, ((0, 8), (1, 64)))
    master = gaussian(seeds[3], (GROUPS, COLS, D), 0.5, 4.0, ((1, 64), (2, 8)), jnp.float32)
    first_mom = gaussian(seeds[4], (GROUPS, COLS, R), 0.3, 2.0, ((0, 8), (1, 64)), jnp.float32)
    second_mom = jnp.clip(jnp.exp(math.log(0.01) - 4.6051702 * jax.random.uniform(seeds[5], (GROUPS, COLS, R), jnp.float32) ** level_of(seeds[5], (GROUPS, COLS, R), ((0, 8), (1, 64)), -0.2, 0.2)), 0.0001, 0.01)
    return {"acts": acts, "grad_out": grad_out, "basis": basis, "master": master, "first_mom": first_mom, "second_mom": second_mom}


beta_one = 0.9
beta_two = 0.999
bias_first = 1.0 - 0.9 ** 10
bias_second = 1.0 - 0.999 ** 10
adam_eps = 1e-08
learn_rate = 0.1

def reference(acts, grad_out, basis, master, first_mom, second_mom):
    projected = jnp.dot(acts, basis, preferred_element_type=jnp.float32).astype(jnp.bfloat16)
    grad = jnp.dot(grad_out.T, projected, preferred_element_type=jnp.float32) * (1.0 / math.sqrt(TOKENS))
    grad = grad.reshape(GROUPS, COLS, R)
    new_first = beta_one * first_mom + (1.0 - beta_one) * grad
    new_second = beta_two * second_mom + (1.0 - beta_two) * grad * grad
    update = (new_first / bias_first / (jnp.sqrt(new_second / bias_second) + adam_eps)).astype(jnp.bfloat16)
    delta = jnp.dot(update.reshape(D, R), basis.T, preferred_element_type=jnp.float32).reshape(GROUPS, COLS, D)
    new_master = master - learn_rate * delta
    forward = new_master.astype(jnp.bfloat16)
    return (new_master, forward, new_first, new_second)
```

```python
import math

import jax
import jax.numpy as jnp
from jax import lax
from jax.sharding import Mesh
from jax.sharding import PartitionSpec as P

beta_one = 0.9
beta_two = 0.999
bias_first = 1.0 - 0.9**10
bias_second = 1.0 - 0.999**10
adam_eps = 1e-08
learn_rate = 0.1

bf16 = jnp.bfloat16
f16 = jnp.float16
f32 = jnp.float32

X, ZL, C, Y, ZH = 4, 8, 2, 4, 2
SWAP = [(0, 1), (1, 0)]


def encode(value):
    return (value * lax.rsqrt(jnp.abs(value) + 1e-30)).astype(f16)


def decode(coded):
    root = coded.astype(f32)
    return root * jnp.abs(root)


def swap(value, axis):
    return lax.ppermute(value, axis, SWAP)


def exchange(value, axis):
    return lax.all_to_all(value, axis, 0, 0)


def gather(value, axis, count):
    return exchange(jnp.broadcast_to(value[None], (count, *value.shape)), axis)


def ordered(first, other, at):
    return jnp.where(at == 0, first, other), jnp.where(at == 0, other, first)


def on_device(acts, grad_out, basis, master, first_mom, second_mom):
    core = lax.axis_index("c")
    high = lax.axis_index("zh")
    tokens = acts.shape[0] * X * ZL * C
    feats = acts.shape[1]
    cols = first_mom.shape[1]
    rank = first_mom.shape[2]
    half = rank // C
    part_rank = basis.shape[1]
    grad_scale = 1.0 / math.sqrt(tokens)

    acts_chip = jnp.concatenate([acts, swap(acts, "c")], 0)
    grad_out_chip = jnp.concatenate([grad_out, swap(grad_out, "c")], 0)

    rows = gather(basis.T, "zl", ZL).reshape(ZL * part_rank, feats)
    rows = gather(rows, "x", X).reshape(half, feats)
    rows_other = swap(rows, "c")

    partial_value = lax.dot_general(
        acts_chip, rows, (((1,), (1,)), ((), ())), preferred_element_type=f32
    )
    quarter = partial_value.shape[0] // Y
    coded = exchange(encode(partial_value).reshape(Y, quarter, half), "y")
    summed = decode(coded).sum(0)
    summed = summed + decode(swap(encode(summed), "zh"))
    projected = gather(summed.astype(bf16), "y", Y).reshape(Y * quarter, half)

    whole = lax.dot_general(
        grad_out_chip, projected, (((0,), (0,)), ((), ())), preferred_element_type=f32
    )
    whole = whole * grad_scale
    block = whole.shape[0] // X
    summed = decode(exchange(encode(whole).reshape(X, block, half), "x")).sum(0)
    coded = exchange(encode(summed).reshape(ZL * C, cols, half), ("zl", "c"))
    grad = decode(coded).reshape(ZL, C, cols, half).sum(0)
    grad = jnp.concatenate([grad[0], grad[1]], 1)

    at = lax.broadcasted_iota(jnp.int32, (rank, rank), 1)
    source = (at % half) // part_rank * (part_rank * C) + at // half * part_rank + at % part_rank
    by_core = (lax.broadcasted_iota(jnp.int32, (rank, rank), 0) == source).astype(f32)

    def permuted(value, dim):
        return lax.dot_general(
            value,
            by_core,
            (((1,), (dim,)), ((), ())),
            precision=lax.Precision.HIGHEST,
            preferred_element_type=f32,
        )

    moments = permuted(jnp.concatenate([first_mom[0], second_mom[0]], 0), 0)
    first = beta_one * moments[:cols] + (1.0 - beta_one) * grad
    second = beta_two * moments[cols:] + (1.0 - beta_two) * grad * grad
    update = (first / bias_first / (jnp.sqrt(second / bias_second) + adam_eps)).astype(bf16)
    moments = permuted(jnp.concatenate([first, second], 0), 1)
    new_first = moments[None, :cols]
    new_second = moments[None, cols:]

    rows_low, rows_high = ordered(rows, rows_other, core)
    rows_all = jnp.concatenate([rows_low, rows_high], 0)
    blocks = master.reshape(Y, ZH, cols, feats)
    master_near, master_far = ordered(blocks[:, 0], blocks[:, 1], high)

    def stepped(updates, old):
        delta = jnp.dot(updates.reshape(Y * cols, rank), rows_all, preferred_element_type=f32)
        new = old.reshape(Y * cols, feats) - learn_rate * delta
        return new, new.astype(bf16)

    update_far = swap(update, "zh")
    near, near_forward = stepped(gather(update, "y", Y), master_near)
    near_of_far = swap(near_forward, "zh")
    far, far_forward = stepped(gather(update_far, "y", Y), master_far)
    far_of_far = swap(far_forward, "zh")

    low, up = ordered(near.reshape(Y, cols, feats), far.reshape(Y, cols, feats), high)
    new_master = jnp.stack([low, up], 1).reshape(master.shape)

    own = gather(jnp.concatenate([near_forward, far_forward], 0), "y", Y)
    own = own.reshape(Y, ZH, Y, cols, feats)
    theirs_far = gather(near_of_far, "y", Y).reshape(Y, Y, cols, feats)
    theirs_near = gather(far_of_far, "y", Y).reshape(Y, Y, cols, feats)
    own_near, own_far = own[:, 0], own[:, 1]
    zero_zero, one_one = ordered(own_near, theirs_far, high)
    one_zero, zero_one = ordered(own_far, theirs_near, high)
    table = jnp.stack(
        [jnp.stack([zero_zero, zero_one], 0), jnp.stack([one_zero, one_one], 0)], 0
    )
    forward = table.transpose(3, 0, 4, 2, 1, 5).reshape(
        master.shape[0], cols, Y * ZH * feats
    )
    return (new_master, forward, new_first, new_second)


def solution(mesh):
    devices = mesh.devices.reshape(X, ZL, C, Y, ZH)
    fine = Mesh(devices, ("x", "zl", "c", "y", "zh"))
    dp = ("x", "zl", "c")
    fsdp = ("y", "zh")
    return jax.shard_map(
        on_device,
        mesh=fine,
        in_specs=(
            P(dp, fsdp),
            P(dp, fsdp),
            P(fsdp, dp),
            P(None, dp, fsdp),
            P(fsdp, dp, None),
            P(fsdp, dp, None),
        ),
        out_specs=(
            P(None, dp, fsdp),
            P(None, dp, None),
            P(fsdp, dp, None),
            P(fsdp, dp, None),
        ),
        check_vma=False,
    )
```

```python
import math

import jax
import jax.numpy as jnp
from jax import lax
from jax.sharding import Mesh
from jax.sharding import PartitionSpec as P

beta_one = 0.9
beta_two = 0.999
bias_first = 1.0 - 0.9**10
bias_second = 1.0 - 0.999**10
adam_eps = 1e-08
learn_rate = 0.1

bf16 = jnp.bfloat16
f16 = jnp.float16
f32 = jnp.float32

X, ZL, C, Y, ZH = 4, 8, 2, 4, 2
ROWS = 8
SWAP = [(0, 1), (1, 0)]


def encode(value):
    return (value * lax.rsqrt(jnp.abs(value) + 1e-30)).astype(f16)


def decode(coded):
    root = coded.astype(f32)
    return root * jnp.abs(root)


def swap(value, axis):
    return lax.ppermute(value, axis, SWAP)


def exchange(value, axis):
    return lax.all_to_all(value, axis, 0, 0)


def gather(value, axis, count):
    return exchange(jnp.broadcast_to(value[None], (count, *value.shape)), axis)


def ordered(first, other, at):
    return jnp.where(at == 0, first, other), jnp.where(at == 0, other, first)


def on_device(acts, grad_out, basis, master, first_mom, second_mom):
    core = lax.axis_index("c")
    high = lax.axis_index("zh")
    tokens = acts.shape[0] * X * ZL * C
    feats = acts.shape[1]
    cols = first_mom.shape[1]
    rank = first_mom.shape[2]
    half = rank // C
    part_rank = basis.shape[1]
    grad_scale = 1.0 / math.sqrt(tokens)

    acts_chip = jnp.concatenate([acts, swap(acts, "c")], 0)
    grad_out_chip = jnp.concatenate([grad_out, swap(grad_out, "c")], 0)

    rows = gather(basis.T, "zl", ZL).reshape(ZL * part_rank, feats)
    rows = gather(rows, "x", X).reshape(half, feats)
    rows_other = swap(rows, "c")

    partial_value = lax.dot_general(
        acts_chip, rows, (((1,), (1,)), ((), ())), preferred_element_type=f32
    )
    quarter = partial_value.shape[0] // Y
    coded = exchange(encode(partial_value).reshape(Y, quarter, half), "y")
    summed = decode(coded).sum(0)
    summed = summed + decode(swap(encode(summed), "zh"))
    projected = gather(summed.astype(bf16), "y", Y).reshape(Y * quarter, half)

    whole = lax.dot_general(
        grad_out_chip, projected, (((0,), (0,)), ((), ())), preferred_element_type=f32
    )
    whole = whole * grad_scale
    block = whole.shape[0] // X
    summed = decode(exchange(encode(whole).reshape(X, block, half), "x")).sum(0)
    coded = exchange(encode(summed).reshape(ZL * C, cols, half), ("zl", "c"))
    grad = decode(coded).reshape(ZL, C, cols, half).sum(0)
    grad = jnp.concatenate([grad[0], grad[1]], 1)

    at = lax.broadcasted_iota(jnp.int32, (rank, rank), 1)
    source = (at % half) // part_rank * (part_rank * C) + at // half * part_rank + at % part_rank
    by_core = (lax.broadcasted_iota(jnp.int32, (rank, rank), 0) == source).astype(f32)

    def permuted(value, dim):
        return lax.dot_general(
            value,
            by_core,
            (((1,), (dim,)), ((), ())),
            precision=lax.Precision.HIGHEST,
            preferred_element_type=f32,
        )

    moments = permuted(jnp.concatenate([first_mom[0], second_mom[0]], 0), 0)
    first = beta_one * moments[:cols] + (1.0 - beta_one) * grad
    second = beta_two * moments[cols:] + (1.0 - beta_two) * grad * grad
    update = (first / bias_first / (jnp.sqrt(second / bias_second) + adam_eps)).astype(bf16)
    moments = permuted(jnp.concatenate([first, second], 0), 1)
    new_first = moments[None, :cols]
    new_second = moments[None, cols:]

    rows_low, rows_high = ordered(rows, rows_other, core)
    rows_all = jnp.concatenate([rows_low, rows_high], 0)
    both = jnp.concatenate([update, swap(update, "zh")], 0)
    updates = gather(both, "y", Y).reshape(Y, ZH, cols, rank)
    low, up = ordered(updates[:, 0], updates[:, 1], high)
    updates = jnp.stack([low, up], 1).reshape(Y * ZH * cols, rank)
    delta = jnp.dot(updates, rows_all, preferred_element_type=f32)
    new_master = master - learn_rate * delta.reshape(master.shape)
    block_forward = new_master.astype(bf16).reshape(Y * ZH * cols, feats)

    tiled = (Y, Y * ZH, cols // ROWS, ROWS, feats)
    here = lax.axis_index("y")
    parts = [block_forward] + [
        lax.ppermute(block_forward, "y", [(i, (i + d) % Y) for i in range(Y)]) for d in (2, 1, 3)
    ]
    far_block = swap(block_forward, "zh")
    *parts, far_block = lax.optimization_barrier((*parts, far_block))
    by_step = [parts[0], parts[2], parts[1], parts[3]]
    stacked = jnp.stack(by_step[::-1] + by_step[::-1], 0)
    own = lax.dynamic_slice_in_dim(stacked, Y - 1 - here, Y, 0)
    theirs = gather(far_block, "y", Y).reshape(tiled)
    forward = jnp.stack(ordered(own.reshape(tiled), theirs, high), 1)
    forward = forward.transpose(2, 3, 4, 0, 1, 5).reshape(
        master.shape[0], cols, Y * ZH * feats
    )
    return (new_master, forward, new_first, new_second)


def solution(mesh):
    devices = mesh.devices.reshape(X, ZL, C, Y, ZH)
    fine = Mesh(devices, ("x", "zl", "c", "y", "zh"))
    dp = ("x", "zl", "c")
    fsdp = ("y", "zh")
    return jax.shard_map(
        on_device,
        mesh=fine,
        in_specs=(
            P(dp, fsdp),
            P(dp, fsdp),
            P(fsdp, dp),
            P(None, dp, fsdp),
            P(fsdp, dp, None),
            P(fsdp, dp, None),
        ),
        out_specs=(
            P(None, dp, fsdp),
            P(None, dp, None),
            P(fsdp, dp, None),
            P(fsdp, dp, None),
        ),
        check_vma=False,
    )
```

```python
import math

import jax
import jax.numpy as jnp
from jax import lax
from jax.sharding import Mesh
from jax.sharding import PartitionSpec as P

beta_one = 0.9
beta_two = 0.999
bias_first = 1.0 - 0.9**10
bias_second = 1.0 - 0.999**10
adam_eps = 1e-08
learn_rate = 0.1

bf16 = jnp.bfloat16
f16 = jnp.float16
f32 = jnp.float32

X, ZL, C, Y, ZH = 4, 8, 2, 4, 2
ROWS = 8
SWAP = [(0, 1), (1, 0)]


def encode(value):
    return (value * lax.rsqrt(jnp.abs(value) + 1e-30)).astype(f16)


def decode(coded):
    root = coded.astype(f32)
    return root * jnp.abs(root)


def swap(value, axis):
    return lax.ppermute(value, axis, SWAP)


def exchange(value, axis):
    return lax.all_to_all(value, axis, 0, 0)


def gather(value, axis, count):
    return exchange(jnp.broadcast_to(value[None], (count, *value.shape)), axis)


def ordered(first, other, at):
    return jnp.where(at == 0, first, other), jnp.where(at == 0, other, first)


def on_device(acts, grad_out, basis, master, first_mom, second_mom):
    core = lax.axis_index("c")
    high = lax.axis_index("zh")
    tokens = acts.shape[0] * X * ZL * C
    feats = acts.shape[1]
    cols = first_mom.shape[1]
    rank = first_mom.shape[2]
    half = rank // C
    part_rank = basis.shape[1]
    grad_scale = 1.0 / math.sqrt(tokens)

    acts_chip = jnp.concatenate([acts, swap(acts, "c")], 0)
    grad_out_chip = jnp.concatenate([grad_out, swap(grad_out, "c")], 0)

    rows = gather(basis.T, "zl", ZL).reshape(ZL * part_rank, feats)
    rows = gather(rows, "x", X).reshape(half, feats)
    rows_other = swap(rows, "c")

    partial_value = lax.dot_general(
        acts_chip, rows, (((1,), (1,)), ((), ())), preferred_element_type=f32
    )
    quarter = partial_value.shape[0] // Y
    coded = exchange(encode(partial_value).reshape(Y, quarter, half), "y")
    summed = decode(coded).sum(0)
    summed = summed + decode(swap(encode(summed), "zh"))
    projected = gather(summed.astype(bf16), "y", Y).reshape(Y * quarter, half)

    whole = lax.dot_general(
        grad_out_chip, projected, (((0,), (0,)), ((), ())), preferred_element_type=f32
    )
    whole = whole * grad_scale
    block = whole.shape[0] // X
    summed = decode(exchange(encode(whole).reshape(X, block, half), "x")).sum(0)
    coded = exchange(encode(summed).reshape(ZL * C, cols, half), ("zl", "c"))
    grad = decode(coded).reshape(ZL, C, cols, half).sum(0)
    grad = jnp.concatenate([grad[0], grad[1]], 1)

    at = lax.broadcasted_iota(jnp.int32, (rank, rank), 1)
    source = (at % half) // part_rank * (part_rank * C) + at // half * part_rank + at % part_rank
    by_core = (lax.broadcasted_iota(jnp.int32, (rank, rank), 0) == source).astype(f32)

    def permuted(value, dim):
        return lax.dot_general(
            value,
            by_core,
            (((1,), (dim,)), ((), ())),
            precision=lax.Precision.HIGHEST,
            preferred_element_type=f32,
        )

    moments = permuted(jnp.concatenate([first_mom[0], second_mom[0]], 0), 0)
    first = beta_one * moments[:cols] + (1.0 - beta_one) * grad
    second = beta_two * moments[cols:] + (1.0 - beta_two) * grad * grad
    update = (first / bias_first / (jnp.sqrt(second / bias_second) + adam_eps)).astype(bf16)
    moments = permuted(jnp.concatenate([first, second], 0), 1)
    new_first = moments[None, :cols]
    new_second = moments[None, cols:]

    rows_low, rows_high = ordered(rows, rows_other, core)
    rows_all = jnp.concatenate([rows_low, rows_high], 0)
    both = jnp.concatenate([update, swap(update, "zh")], 0)
    updates = gather(both, "y", Y).reshape(Y, ZH, cols, rank)
    low, up = ordered(updates[:, 0], updates[:, 1], high)
    updates = jnp.stack([low, up], 1).reshape(Y * ZH * cols, rank)
    delta = jnp.dot(updates, rows_all, preferred_element_type=f32)
    new_master = master - learn_rate * delta.reshape(master.shape)
    block_forward = new_master.astype(bf16).reshape(Y * ZH * cols, feats)

    tiled = (Y, Y * ZH, cols // ROWS, ROWS, feats)
    here = lax.axis_index("y")
    parts = [block_forward] + [
        lax.ppermute(block_forward, "y", [(i, (i + d) % Y) for i in range(Y)]) for d in (2, 1, 3)
    ]
    far_block = swap(block_forward, "zh")
    *parts, far_block = lax.optimization_barrier((*parts, far_block))
    by_step = [parts[0], parts[2], parts[1], parts[3]]
    stacked = jnp.stack(by_step[::-1] + by_step[::-1], 0)
    own = lax.dynamic_slice_in_dim(stacked, Y - 1 - here, Y, 0)
    theirs = gather(far_block, "y", Y)

    def tiles(block):
        return block.reshape(tiled).transpose(1, 2, 0, 3, 4)[:, :, :, None]

    table = jnp.zeros((Y * ZH, cols // ROWS, Y, ZH, ROWS, feats), bf16)
    table = lax.dynamic_update_slice(table, tiles(own), (0, 0, 0, high, 0, 0))
    table = lax.dynamic_update_slice(table, tiles(theirs), (0, 0, 0, 1 - high, 0, 0))
    forward = table.transpose(0, 1, 4, 2, 3, 5).reshape(
        master.shape[0], cols, Y * ZH * feats
    )
    return (new_master, forward, new_first, new_second)


def solution(mesh):
    devices = mesh.devices.reshape(X, ZL, C, Y, ZH)
    fine = Mesh(devices, ("x", "zl", "c", "y", "zh"))
    dp = ("x", "zl", "c")
    fsdp = ("y", "zh")
    return jax.shard_map(
        on_device,
        mesh=fine,
        in_specs=(
            P(dp, fsdp),
            P(dp, fsdp),
            P(fsdp, dp),
            P(None, dp, fsdp),
            P(fsdp, dp, None),
            P(fsdp, dp, None),
        ),
        out_specs=(
            P(None, dp, fsdp),
            P(None, dp, None),
            P(fsdp, dp, None),
            P(fsdp, dp, None),
        ),
        check_vma=False,
    )
```

```python
import math

import jax
import jax.numpy as jnp
from jax import lax
from jax.sharding import Mesh
from jax.sharding import PartitionSpec as P

beta_one = 0.9
beta_two = 0.999
bias_first = 1.0 - 0.9**10
bias_second = 1.0 - 0.999**10
adam_eps = 1e-08
learn_rate = 0.1

bf16 = jnp.bfloat16
f16 = jnp.float16
f32 = jnp.float32

X, ZL, C, Y, ZH = 4, 8, 2, 4, 2
ROWS = 8
SWAP = [(0, 1), (1, 0)]


root_scale = 32.0


def encode(value):
    return (value * (root_scale * lax.rsqrt(jnp.abs(value) + 1e-30))).astype(f16)


def decode(coded):
    root = coded.astype(f32) * (1.0 / root_scale)
    return root * jnp.abs(root)


def swap(value, axis):
    return lax.ppermute(value, axis, SWAP)


def exchange(value, axis):
    return lax.all_to_all(value, axis, 0, 0)


def gather(value, axis, count):
    return exchange(jnp.broadcast_to(value[None], (count, *value.shape)), axis)


def ordered(first, other, at):
    return jnp.where(at == 0, first, other), jnp.where(at == 0, other, first)


def on_device(acts, grad_out, basis, master, first_mom, second_mom):
    core = lax.axis_index("c")
    high = lax.axis_index("zh")
    tokens = acts.shape[0] * X * ZL * C
    feats = acts.shape[1]
    cols = first_mom.shape[1]
    rank = first_mom.shape[2]
    half = rank // C
    part_rank = basis.shape[1]
    grad_scale = 1.0 / math.sqrt(tokens)

    acts_chip = jnp.concatenate([acts, swap(acts, "c")], 0)
    grad_out_chip = jnp.concatenate([grad_out, swap(grad_out, "c")], 0)

    rows = gather(basis.T, "zl", ZL).reshape(ZL * part_rank, feats)
    rows = gather(rows, "x", X).reshape(half, feats)
    rows_other = swap(rows, "c")

    partial_value = lax.dot_general(
        acts_chip, rows, (((1,), (1,)), ((), ())), preferred_element_type=f32
    )
    quarter = partial_value.shape[0] // Y
    coded = exchange(encode(partial_value).reshape(Y, quarter, half), "y")
    summed = decode(coded).sum(0)
    summed = summed + decode(swap(encode(summed), "zh"))
    projected = gather(summed.astype(bf16), "y", Y).reshape(Y * quarter, half)

    whole = lax.dot_general(
        grad_out_chip, projected, (((0,), (0,)), ((), ())), preferred_element_type=f32
    )
    whole = whole * grad_scale
    block = whole.shape[0] // X
    summed = decode(exchange(encode(whole).reshape(X, block, half), "x")).sum(0)
    coded = exchange(encode(summed).reshape(ZL * C, cols, half), ("zl", "c"))
    grad = decode(coded).reshape(ZL, C, cols, half).sum(0)
    grad = jnp.concatenate([grad[0], grad[1]], 1)

    at = lax.broadcasted_iota(jnp.int32, (rank, rank), 1)
    source = (at % half) // part_rank * (part_rank * C) + at // half * part_rank + at % part_rank
    by_core = (lax.broadcasted_iota(jnp.int32, (rank, rank), 0) == source).astype(f32)

    def permuted(value, dim):
        return lax.dot_general(
            value,
            by_core,
            (((1,), (dim,)), ((), ())),
            precision=lax.Precision.HIGHEST,
            preferred_element_type=f32,
        )

    moments = permuted(jnp.concatenate([first_mom[0], second_mom[0]], 0), 0)
    first = beta_one * moments[:cols] + (1.0 - beta_one) * grad
    second = beta_two * moments[cols:] + (1.0 - beta_two) * grad * grad
    update = (first / bias_first / (jnp.sqrt(second / bias_second) + adam_eps)).astype(bf16)
    moments = permuted(jnp.concatenate([first, second], 0), 1)
    new_first = moments[None, :cols]
    new_second = moments[None, cols:]

    rows_low, rows_high = ordered(rows, rows_other, core)
    rows_all = jnp.concatenate([rows_low, rows_high], 0)
    both = jnp.concatenate([update, swap(update, "zh")], 0)
    updates = gather(both, "y", Y).reshape(Y, ZH, cols, rank)
    low, up = ordered(updates[:, 0], updates[:, 1], high)
    updates = jnp.stack([low, up], 1).reshape(Y * ZH * cols, rank)
    delta = jnp.dot(updates, rows_all, preferred_element_type=f32)
    new_master = master - learn_rate * delta.reshape(master.shape)
    block_forward = new_master.astype(bf16).reshape(Y * ZH * cols, feats)

    tiled = (Y, Y * ZH, cols // ROWS, ROWS, feats)
    here = lax.axis_index("y")
    parts = [block_forward] + [
        lax.ppermute(block_forward, "y", [(i, (i + d) % Y) for i in range(Y)]) for d in (2, 1, 3)
    ]
    far_block = swap(block_forward, "zh")
    *parts, far_block = lax.optimization_barrier((*parts, far_block))
    by_step = [parts[0], parts[2], parts[1], parts[3]]
    stacked = jnp.stack(by_step[::-1] + by_step[::-1], 0)
    own = lax.dynamic_slice_in_dim(stacked, Y - 1 - here, Y, 0)
    theirs = gather(far_block, "y", Y)

    def tiles(block):
        return block.reshape(tiled).transpose(1, 2, 0, 3, 4)[:, :, :, None]

    table = jnp.zeros((Y * ZH, cols // ROWS, Y, ZH, ROWS, feats), bf16)
    table = lax.dynamic_update_slice(table, tiles(own), (0, 0, 0, high, 0, 0))
    table = lax.dynamic_update_slice(table, tiles(theirs), (0, 0, 0, 1 - high, 0, 0))
    forward = table.transpose(0, 1, 4, 2, 3, 5).reshape(
        master.shape[0], cols, Y * ZH * feats
    )
    return (new_master, forward, new_first, new_second)


def solution(mesh):
    devices = mesh.devices.reshape(X, ZL, C, Y, ZH)
    fine = Mesh(devices, ("x", "zl", "c", "y", "zh"))
    dp = ("x", "zl", "c")
    fsdp = ("y", "zh")
    return jax.shard_map(
        on_device,
        mesh=fine,
        in_specs=(
            P(dp, fsdp),
            P(dp, fsdp),
            P(fsdp, dp),
            P(None, dp, fsdp),
            P(fsdp, dp, None),
            P(fsdp, dp, None),
        ),
        out_specs=(
            P(None, dp, fsdp),
            P(None, dp, None),
            P(fsdp, dp, None),
            P(fsdp, dp, None),
        ),
        check_vma=False,
    )
```

```python
import math

import jax
import jax.numpy as jnp
from jax import lax
from jax.sharding import Mesh
from jax.sharding import PartitionSpec as P

beta_one = 0.9
beta_two = 0.999
bias_first = 1.0 - 0.9**10
bias_second = 1.0 - 0.999**10
adam_eps = 1e-08
learn_rate = 0.1

bf16 = jnp.bfloat16
f16 = jnp.float16
f32 = jnp.float32

X, ZL, C, Y, ZH = 4, 8, 2, 4, 2
ROWS = 8
SWAP = [(0, 1), (1, 0)]


root_scale = 32.0


def encode(value):
    return (value * (root_scale * lax.rsqrt(jnp.abs(value) + 1e-30))).astype(f16)


def decode(coded):
    root = coded.astype(f32) * (1.0 / root_scale)
    return root * jnp.abs(root)


def swap(value, axis):
    return lax.ppermute(value, axis, SWAP)


def exchange(value, axis):
    return lax.all_to_all(value, axis, 0, 0)


def gather(value, axis, count):
    return exchange(jnp.broadcast_to(value[None], (count, *value.shape)), axis)


def ordered(first, other, at):
    return jnp.where(at == 0, first, other), jnp.where(at == 0, other, first)


def on_device(acts, grad_out, basis, master, first_mom, second_mom):
    core = lax.axis_index("c")
    high = lax.axis_index("zh")
    tokens = acts.shape[0] * X * ZL * C
    feats = acts.shape[1]
    cols = first_mom.shape[1]
    rank = first_mom.shape[2]
    half = rank // C
    part_rank = basis.shape[1]
    grad_scale = 1.0 / math.sqrt(tokens)

    acts_chip = jnp.concatenate([acts, swap(acts, "c")], 0)
    grad_out_chip = jnp.concatenate([grad_out, swap(grad_out, "c")], 0)

    rows = gather(basis.T, "zl", ZL).reshape(ZL * part_rank, feats)
    rows = gather(rows, "x", X).reshape(half, feats)
    rows_other = swap(rows, "c")

    partial_value = lax.dot_general(
        acts_chip, rows, (((1,), (1,)), ((), ())), preferred_element_type=f32
    )
    quarter = partial_value.shape[0] // Y
    coded = exchange(encode(partial_value).reshape(Y, quarter, half), "y")
    summed = decode(coded).sum(0)
    summed = summed + decode(swap(encode(summed), "zh"))
    projected = gather(summed.astype(bf16), "y", Y).reshape(Y * quarter, half)

    whole = lax.dot_general(
        grad_out_chip, projected, (((0,), (0,)), ((), ())), preferred_element_type=f32
    )
    whole = whole * grad_scale
    block = whole.shape[0] // X
    summed = decode(exchange(encode(whole).reshape(X, block, half), "x")).sum(0)
    coded = exchange(encode(summed).reshape(ZL * C, cols, half), ("zl", "c"))
    grad = decode(coded).reshape(ZL, C, cols, half).sum(0)
    grad = jnp.concatenate([grad[0], grad[1]], 1)

    at = lax.broadcasted_iota(jnp.int32, (rank, rank), 1)
    source = (at % half) // part_rank * (part_rank * C) + at // half * part_rank + at % part_rank
    by_core = (lax.broadcasted_iota(jnp.int32, (rank, rank), 0) == source).astype(f32)

    def permuted(value, dim):
        return lax.dot_general(
            value,
            by_core,
            (((1,), (dim,)), ((), ())),
            precision=lax.Precision.HIGHEST,
            preferred_element_type=f32,
        )

    moments = permuted(jnp.concatenate([first_mom[0], second_mom[0]], 0), 0)
    first = beta_one * moments[:cols] + (1.0 - beta_one) * grad
    second = beta_two * moments[cols:] + (1.0 - beta_two) * grad * grad
    update = (first / bias_first / (jnp.sqrt(second / bias_second) + adam_eps)).astype(bf16)
    moments = permuted(jnp.concatenate([first, second], 0), 1)
    new_first = moments[None, :cols]
    new_second = moments[None, cols:]

    rows_low, rows_high = ordered(rows, rows_other, core)
    rows_all = jnp.concatenate([rows_low, rows_high], 0)
    both = jnp.concatenate(ordered(update, swap(update, "zh"), high), 0)
    updates = gather(both, "y", Y).reshape(Y * ZH * cols, rank)
    delta = jnp.dot(updates, rows_all, preferred_element_type=f32)
    new_master = master - learn_rate * delta.reshape(master.shape)
    block_forward = new_master.astype(bf16).reshape(Y * ZH * cols, feats)

    tiled = (Y, Y * ZH, cols // ROWS, ROWS, feats)
    here = lax.axis_index("y")
    parts = [block_forward] + [
        lax.ppermute(block_forward, "y", [(i, (i + d) % Y) for i in range(Y)]) for d in (2, 1, 3)
    ]
    far_block = swap(block_forward, "zh")
    *parts, far_block = lax.optimization_barrier((*parts, far_block))
    by_step = [parts[0], parts[2], parts[1], parts[3]]
    stacked = jnp.stack(by_step[::-1] + by_step[::-1], 0)
    own = lax.dynamic_slice_in_dim(stacked, Y - 1 - here, Y, 0)
    theirs = gather(far_block, "y", Y)

    def tiles(block):
        return block.reshape(tiled).transpose(1, 2, 0, 3, 4)[:, :, :, None]

    table = jnp.zeros((Y * ZH, cols // ROWS, Y, ZH, ROWS, feats), bf16)
    table = lax.dynamic_update_slice(table, tiles(own), (0, 0, 0, high, 0, 0))
    table = lax.dynamic_update_slice(table, tiles(theirs), (0, 0, 0, 1 - high, 0, 0))
    forward = table.transpose(0, 1, 4, 2, 3, 5).reshape(
        master.shape[0], cols, Y * ZH * feats
    )
    return (new_master, forward, new_first, new_second)


def solution(mesh):
    devices = mesh.devices.reshape(X, ZL, C, Y, ZH)
    fine = Mesh(devices, ("x", "zl", "c", "y", "zh"))
    dp = ("x", "zl", "c")
    fsdp = ("y", "zh")
    return jax.shard_map(
        on_device,
        mesh=fine,
        in_specs=(
            P(dp, fsdp),
            P(dp, fsdp),
            P(fsdp, dp),
            P(None, dp, fsdp),
            P(fsdp, dp, None),
            P(fsdp, dp, None),
        ),
        out_specs=(
            P(None, dp, fsdp),
            P(None, dp, None),
            P(fsdp, dp, None),
            P(fsdp, dp, None),
        ),
        check_vma=False,
    )
```

```python
import math

import jax
import jax.numpy as jnp
from jax import lax
from jax.sharding import Mesh
from jax.sharding import PartitionSpec as P

beta_one = 0.9
beta_two = 0.999
bias_first = 1.0 - 0.9**10
bias_second = 1.0 - 0.999**10
adam_eps = 1e-08
learn_rate = 0.1

bf16 = jnp.bfloat16
f16 = jnp.float16
f32 = jnp.float32

X, ZL, C, Y, ZH = 4, 8, 2, 4, 2
ROWS = 8
SWAP = [(0, 1), (1, 0)]


root_scale = 32.0


def encode(value):
    return (value * (root_scale * lax.rsqrt(jnp.abs(value) + 1e-30))).astype(f16)


def decode(coded):
    root = coded.astype(f32) * (1.0 / root_scale)
    return root * jnp.abs(root)


def swap(value, axis):
    return lax.ppermute(value, axis, SWAP)


def exchange(value, axis):
    return lax.all_to_all(value, axis, 0, 0)


def gather(value, axis, count):
    return exchange(jnp.broadcast_to(value[None], (count, *value.shape)), axis)


def ordered(first, other, at):
    return jnp.where(at == 0, first, other), jnp.where(at == 0, other, first)


def on_device(acts, grad_out, basis, master, first_mom, second_mom):
    core = lax.axis_index("c")
    high = lax.axis_index("zh")
    tokens = acts.shape[0] * X * ZL * C
    feats = acts.shape[1]
    cols = first_mom.shape[1]
    rank = first_mom.shape[2]
    half = rank // C
    part_rank = basis.shape[1]
    grad_scale = 1.0 / math.sqrt(tokens)

    acts_chip = jnp.concatenate([acts, swap(acts, "c")], 0)
    grad_out_chip = jnp.concatenate([grad_out, swap(grad_out, "c")], 0)

    rows = gather(basis.T, "zl", ZL).reshape(ZL * part_rank, feats)
    rows = gather(rows, "x", X).reshape(half, feats)
    rows_other = swap(rows, "c")

    partial_value = lax.dot_general(
        acts_chip, rows, (((1,), (1,)), ((), ())), preferred_element_type=f32
    )
    quarter = partial_value.shape[0] // Y
    coded = exchange(encode(partial_value).reshape(Y, quarter, half), "y")
    summed = decode(coded).sum(0)
    summed = summed + decode(swap(encode(summed), "zh"))
    projected = gather(summed.astype(bf16), "y", Y).reshape(Y * quarter, half)

    whole = lax.dot_general(
        grad_out_chip, projected, (((0,), (0,)), ((), ())), preferred_element_type=f32
    )
    whole = whole * grad_scale
    block = whole.shape[0] // X
    summed = decode(exchange(encode(whole).reshape(X, block, half), "x")).sum(0)
    coded = exchange(encode(summed).reshape(ZL * C, cols, half), ("zl", "c"))
    grad = decode(coded).reshape(ZL, C, cols, half).sum(0)
    grad = jnp.concatenate([grad[0], grad[1]], 1)

    at = lax.broadcasted_iota(jnp.int32, (rank, rank), 1)
    source = (at % half) // part_rank * (part_rank * C) + at // half * part_rank + at % part_rank
    by_core = (lax.broadcasted_iota(jnp.int32, (rank, rank), 0) == source).astype(f32)

    def permuted(value, dim):
        return lax.dot_general(
            value,
            by_core,
            (((1,), (dim,)), ((), ())),
            precision=lax.Precision.HIGHEST,
            preferred_element_type=f32,
        )

    moments = permuted(jnp.concatenate([first_mom[0], second_mom[0]], 0), 0)
    first = beta_one * moments[:cols] + (1.0 - beta_one) * grad
    second = beta_two * moments[cols:] + (1.0 - beta_two) * grad * grad
    update = (first / bias_first / (jnp.sqrt(second / bias_second) + adam_eps)).astype(bf16)
    moments = permuted(jnp.concatenate([first, second], 0), 1)
    new_first = moments[None, :cols]
    new_second = moments[None, cols:]

    rows_low, rows_high = ordered(rows, rows_other, core)
    rows_all = jnp.concatenate([rows_low, rows_high], 0)
    both = jnp.concatenate([update, swap(update, "zh")], 0)
    updates = gather(both, "y", Y).reshape(Y, ZH, cols, rank)
    low, up = ordered(updates[:, 0], updates[:, 1], high)
    updates = jnp.stack([low, up], 1).reshape(Y * ZH * cols, rank)
    delta = jnp.dot(updates, rows_all, preferred_element_type=f32)
    new_master = master - learn_rate * delta.reshape(master.shape)
    block_forward = new_master.astype(bf16).reshape(Y * ZH * cols, feats)

    tiled = (Y, Y * ZH, cols // ROWS, ROWS, feats)
    here = lax.axis_index("y")
    parts = [block_forward] + [
        lax.ppermute(block_forward, "y", [(i, (i + d) % Y) for i in range(Y)]) for d in (1, 3, 2)
    ]
    far_block = swap(block_forward, "zh")
    *parts, far_block = lax.optimization_barrier((*parts, far_block))
    by_step = [parts[0], parts[1], parts[3], parts[2]]
    stacked = jnp.stack(by_step[::-1] + by_step[::-1], 0)
    own = lax.dynamic_slice_in_dim(stacked, Y - 1 - here, Y, 0)
    theirs = gather(far_block, "y", Y)

    def tiles(block):
        return block.reshape(tiled).transpose(1, 2, 0, 3, 4)[:, :, :, None]

    table = jnp.zeros((Y * ZH, cols // ROWS, Y, ZH, ROWS, feats), bf16)
    table = lax.dynamic_update_slice(table, tiles(own), (0, 0, 0, high, 0, 0))
    table = lax.dynamic_update_slice(table, tiles(theirs), (0, 0, 0, 1 - high, 0, 0))
    forward = table.transpose(0, 1, 4, 2, 3, 5).reshape(
        master.shape[0], cols, Y * ZH * feats
    )
    return (new_master, forward, new_first, new_second)


def solution(mesh):
    devices = mesh.devices.reshape(X, ZL, C, Y, ZH)
    fine = Mesh(devices, ("x", "zl", "c", "y", "zh"))
    dp = ("x", "zl", "c")
    fsdp = ("y", "zh")
    return jax.shard_map(
        on_device,
        mesh=fine,
        in_specs=(
            P(dp, fsdp),
            P(dp, fsdp),
            P(fsdp, dp),
            P(None, dp, fsdp),
            P(fsdp, dp, None),
            P(fsdp, dp, None),
        ),
        out_specs=(
            P(None, dp, fsdp),
            P(None, dp, None),
            P(fsdp, dp, None),
            P(fsdp, dp, None),
        ),
        check_vma=False,
    )
```
